32 devices in a mesh: rep: 4 (over y, core), fsdp: 8 (over z, x).
Axes of the slice: x: 2, y: 2, z: 4, core: 2. Of those that a mesh axis runs over, the one named last changes fastest.
Arguments:
- grad: bfloat16 [4, 4096, 8192], P('rep', 'fsdp'), may hold values from -12 to 12
- error: float32 [4, 4096, 8192], P('rep', 'fsdp'), may hold values from -2 to 2
- q_prev: float32 [8192, 32], replicated, may hold values from -6 to 6
Outputs:
- update: bfloat16 [4096, 8192], P('fsdp')
- new_error: float32 [4, 4096, 8192], P('rep', 'fsdp')
- q_next: float32 [8192, 32], replicated
The draws below stay inside these ranges and needn't reach their ends.
All inputs are finite; a program needn't handle non-finite values.
Results may differ from the reference program's by a relative error of at most 0.001.
Values sent between devices are 32-bit elements; how exact they have to be, the bound alone decides.
No kernel may reach another device: no remote copies, remote signals or barrier semaphores. Data moves between devices by JAX's collectives and lax.ppermute only.
A program may use at most 128 MiB of HBM per device.

```python
import math
import jax
import jax.numpy as jnp
from jax import lax

D = 4096
FFW = 8192
RANK = 32
REPLICAS = 4


def draw_grad(key, part):
    key = jax.random.fold_in(key, 11)
    keys = jax.random.split(key, 3)
    rows = jnp.arange(D, dtype=jnp.float32) / D
    row_scale = jnp.exp(math.log(3.0) * rows + jax.random.uniform(keys[0], (D,), jnp.float32, -1.15, 1.15))
    col_scale = jnp.exp(jax.random.uniform(keys[1], (FFW,), jnp.float32, -1.15, 1.15))
    base = jnp.clip(jax.random.normal(keys[2], (REPLICAS, D, FFW), jnp.float32), -4.0, 4.0)
    values = 0.1 * base * row_scale[None, :, None] * col_scale[None, None, :]
    return values.astype(jnp.bfloat16)


def block_scale(rng, dims, shards, low, largest):
    factor_of, own = 1.0, jax.random.fold_in(rng, 6)
    for dim, parts in shards:
        heights = jnp.exp(jax.random.uniform(jax.random.fold_in(own, dim), (parts,), jnp.float32, low / len(shards), largest / len(shards)))
        factor_of = factor_of * jnp.repeat(heights, dims[dim] // parts).reshape([-1 if axis == dim else 1 for axis in range(len(dims))])
    return factor_of


def centred(key, dims, spread, most, cuts=(), held_as=jnp.bfloat16):
    level = block_scale(key, dims, cuts, -0.22, 0.18) if cuts else 1.0
    entries = jax.random.normal(key, dims, jnp.float32) * spread * level
    return jnp.minimum(jnp.maximum(entries, -most), most).astype(held_as)


def setup_inputs(seed: int = 0) -> dict:
    key_list = jax.random.split(jax.random.key(seed), 4)
    grad = draw_grad(jax.random.fold_in(key_list[3], 71), 0)
    error = centred(key_list[1], (REPLICAS, D, FFW), 0.3, 2.0, ((0, 4), (1, 8)), jnp.float32)
    q_prev = centred(key_list[2], (FFW, RANK), 1.0, 6.0, (), jnp.float32)
    return dict(grad=grad, error=error, q_prev=q_prev)


def reference(grad, error, q_prev):
    highest = lax.Precision.HIGHEST
    corrected = grad.astype(jnp.float32) + error
    p_mean = jnp.einsum('rdf,fk->dk', corrected, q_prev, precision=highest) / REPLICAS
    gram = jnp.dot(p_mean.T, p_mean, precision=highest)
    shift = 0.001 * jnp.trace(gram) / RANK
    shifted = gram + shift * jnp.eye(RANK, dtype=jnp.float32)
    chol = jnp.linalg.cholesky(shifted)
    p_hat = lax.linalg.triangular_solve(chol, p_mean, left_side=False, lower=True, transpose_a=True)
    q_next = jnp.einsum('rdf,dk->fk', corrected, p_hat, precision=highest) / REPLICAS
    approx = jnp.dot(p_hat, q_next.T, precision=highest)
    update = approx.astype(jnp.bfloat16)
    new_error = corrected - approx[None]
    return (update, new_error, q_next)
```

```python
import functools

import jax
import jax.numpy as jnp
from jax import lax
from jax.experimental import pallas as pl
from jax.experimental.pallas import tpu as pltpu
from jax.sharding import PartitionSpec as P

F32, BF16 = jnp.float32, jnp.bfloat16
HIGHEST = lax.Precision.HIGHEST
AXES = ("rep", "fsdp")
NT = (((1,), (1,)), ((), ()))
NN = (((1,), (0,)), ((), ()))
VMEM = pl.BlockSpec(memory_space=pltpu.VMEM)
PIECES = 32
GRAM_LANES = 128


def params(mib):
    return pltpu.CompilerParams(vmem_limit_bytes=mib * 2**20)


def in_vmem(x):
    return pltpu.with_memory_space_constraint(x, pltpu.VMEM)


def in_hbm(x):
    return pltpu.with_memory_space_constraint(x, pltpu.HBM)


def two(x):
    high = x.astype(BF16)
    return high, (x - high.astype(F32)).astype(BF16)


def dot(a, b, dims=NN, precision=None):
    return lax.dot_general(a, b, dims, precision=precision, preferred_element_type=F32)


def correct_kernel(parts, place, grad, error, qt, high, low, pt, grads, errors, factors, total, sems, q_sem):
    rows, cols = high.shape
    rank = qt.shape[0]
    width = cols // parts
    take_q = pltpu.make_async_copy(qt, factors, q_sem)
    take_q.start()
    takes = []
    for part in range(parts):
        columns = pl.ds(part * width, width)
        takes.append(
            (
                pltpu.make_async_copy(error.at[0, :, columns], errors.at[:, columns], sems.at[0, part]),
                pltpu.make_async_copy(grad.at[0, :, columns], grads.at[:, columns], sems.at[1, part]),
            )
        )
        for take in takes[-1]:
            take.start()
    total[...] = jnp.zeros_like(total)
    take_q.wait()
    for part in range(parts):
        columns = pl.ds(part * width, width)
        for take in takes[part]:
            take.wait()
        hi, lo = two(grads[:, columns].astype(F32) + errors[:, columns])
        high[:, columns] = hi
        low[:, columns] = lo
        qh, ql = two(factors[:, columns])
        a = dot(jnp.concatenate([qh, ql], 0), hi, NT)
        total[...] += a[:rank] + a[rank:] + dot(qh, lo, NT)
    pt[...] = total[...]


def correct(place, grad, error, qt):
    _, rows, cols = grad.shape
    rank = qt.shape[0]
    parts = cols // 512
    return pl.pallas_call(
        functools.partial(correct_kernel, parts),
        in_specs=[pl.BlockSpec(memory_space=pltpu.SMEM)] + [pl.BlockSpec(memory_space=pltpu.HBM)] * 3,
        out_specs=[VMEM, VMEM, VMEM],
        out_shape=[
            pltpu.VMEM((rows, cols), BF16),
            pltpu.VMEM((rows, cols), BF16),
            pltpu.VMEM((rank, rows), F32),
        ],
        scratch_shapes=[
            pltpu.VMEM((rows, cols), BF16),
            pltpu.VMEM((rows, cols), F32),
            pltpu.VMEM((rank, cols), F32),
            pltpu.VMEM((rank, rows), F32),
            pltpu.SemaphoreType.DMA((2, parts)),
            pltpu.SemaphoreType.DMA,
        ],
        compiler_params=params(32),
        name="correct",
    )(place, in_hbm(grad), in_hbm(error), in_hbm(qt))


def terms_kernel(replicas, first, place, pt, high, low, terms, gram, mean):
    pieces, rank, width = terms.shape
    pm = pt[...] / replicas
    if gram is not None:
        mean[...] = pm
        gram[...] = jnp.zeros_like(gram)
        gram[:, :rank] = dot(pm, pm, NT, HIGHEST)
    ph, pl_ = two(pm)
    both = jnp.concatenate([ph, pl_], 0)
    here = place[0]

    def body(n, carry):
        columns = pl.ds(pl.multiple_of(((n + first) ^ here) * width, width), width)
        a = dot(both, high[:, columns])
        terms[n] = a[:rank] + a[rank:] + dot(ph, low[:, columns])
        return carry

    lax.fori_loop(0, pieces, body, 0, unroll=4)


def terms_of(place, pt, high, low, replicas, first, pieces, with_gram):
    rank, rows = pt.shape
    width = high.shape[1] // PIECES
    kernel = functools.partial(terms_kernel, replicas, first)
    shapes = [pltpu.VMEM((pieces, rank, width), F32)]
    if with_gram:
        shapes += [pltpu.VMEM((rank, GRAM_LANES), F32), pltpu.VMEM((rank, rows), F32)]
    return pl.pallas_call(
        kernel if with_gram else lambda *refs: kernel(*refs, None, None),
        in_specs=[pl.BlockSpec(memory_space=pltpu.SMEM), VMEM, VMEM, VMEM],
        out_specs=[VMEM] * len(shapes),
        out_shape=shapes,
        compiler_params=params(8),
        name="terms",
    )(place, pt, in_vmem(high), in_vmem(low))


def factor_kernel(gram, mean, inverse, left):
    rank = mean.shape[0]
    rows = mean.shape[1]
    i = lax.broadcasted_iota(jnp.int32, (rank, GRAM_LANES), 0)
    j = lax.broadcasted_iota(jnp.int32, (rank, GRAM_LANES), 1)
    total = gram[...]
    diagonal = jnp.where(i == j, total, 0.0)
    trace = jnp.sum(jnp.sum(diagonal, 1, keepdims=True), 0, keepdims=True)
    shift = 0.001 * trace / rank
    work = total + jnp.where(i == j, shift, 0.0) + jnp.where(j == i + rank, 1.0, 0.0)
    scale = jnp.zeros((rank, 1), F32)
    row_of = lax.broadcasted_iota(jnp.int32, (rank, 1), 0)
    for k in range(rank):
        pivot = work[k : k + 1, :]
        value = pivot[:, k : k + 1]
        scale = jnp.where(row_of == k, lax.rsqrt(value), scale)
        if k + 1 < rank:
            factor = jnp.where(row_of > k, work[:, k : k + 1] / value, 0.0)
            work = work - factor * pivot
    w = work[:, rank : 2 * rank] * scale
    inverse[...] = w
    hat = dot(w, mean[...], NN, HIGHEST).T
    h, l = two(hat)
    left[...] = jnp.concatenate([h, l, h, jnp.zeros((rows, 128 - 3 * rank), BF16)], 1)


def factor(gram, mean):
    rank, rows = mean.shape
    return pl.pallas_call(
        factor_kernel,
        in_specs=[VMEM, VMEM],
        out_specs=[VMEM, VMEM],
        out_shape=[pltpu.VMEM((rank, rank), F32), pltpu.VMEM((rows, 128), BF16)],
        compiler_params=params(8),
        name="factor",
    )(gram, mean)


def update_kernel(replicas, place, sums, inverse, left, high, low, new_error, update, qt, errors, updates, factors, right, sems):
    rank, width = sums.shape[1:]
    groups = errors.shape[0]
    each = sums.shape[0] // groups
    span = each * width
    group_here, piece_here = place[0] // each, place[0] % each
    right[3 * rank :, :] = jnp.zeros((128 - 3 * rank, right.shape[1]), BF16)
    for g in range(groups):
        for n in range(each):
            at = g * each + n
            q = dot(inverse[...], sums[at], NN, HIGHEST) / replicas
            factors[g, :, pl.ds(pl.multiple_of((n ^ piece_here) * width, width), width)] = q
            h, l = two(q)
            right[: 3 * rank, at * width : (at + 1) * width] = jnp.concatenate([h, h, l], 0)
    gives = []
    for g in range(groups):
        start = (g ^ group_here) * span
        for n in range(each):
            at = g * each + n
            inner = pl.multiple_of((n ^ piece_here) * width, width)
            columns = pl.ds(pl.multiple_of(start + inner, width), width)
            approx = dot(left[...], right[:, at * width : (at + 1) * width])
            updates[g, :, pl.ds(inner, width)] = approx.astype(BF16)
            errors[g, :, pl.ds(inner, width)] = (high[:, columns].astype(F32) - approx) + low[:, columns].astype(F32)
        columns = pl.ds(pl.multiple_of(start, span), span)
        for k, (source, target) in enumerate(
            ((errors.at[g], new_error.at[0, :, columns]), (updates.at[g], update.at[:, columns]), (factors.at[g], qt.at[:, columns]))
        ):
            gives.append(pltpu.make_async_copy(source, target, sems.at[k, g]))
            gives[-1].start()
    for give in gives:
        give.wait()


def update_of(place, sums, inverse, left, high, low, replicas):
    pieces, rank, width = sums.shape
    rows, cols = high.shape
    each = 4
    groups = pieces // each
    return pl.pallas_call(
        functools.partial(update_kernel, replicas),
        in_specs=[pl.BlockSpec(memory_space=pltpu.SMEM)] + [VMEM] * 5,
        out_specs=[pl.BlockSpec(memory_space=pltpu.HBM)] * 3,
        out_shape=[
            jax.ShapeDtypeStruct((1, rows, cols), F32),
            jax.ShapeDtypeStruct((rows, cols), BF16),
            jax.ShapeDtypeStruct((rank, cols), F32),
        ],
        scratch_shapes=[
            pltpu.VMEM((groups, rows, each * width), F32),
            pltpu.VMEM((groups, rows, each * width), BF16),
            pltpu.VMEM((groups, rank, each * width), F32),
            pltpu.VMEM((128, pieces * width), BF16),
            pltpu.SemaphoreType.DMA((3, groups)),
        ],
        compiler_params=params(32),
        name="update",
    )(place, sums, inverse, left, in_vmem(high), in_vmem(low))


def swap(x, mask):
    devices = lax.axis_size("rep") * lax.axis_size("fsdp")
    return lax.ppermute(x, AXES, [(i, i ^ mask) for i in range(devices)])


CORE, Y, X, Z_LOW, Z_HIGH = 8, 16, 1, 2, 4


def all_sum(kept, given, gram):
    rank, width = kept.shape[1:]
    gram = jnp.pad(gram, ((0, 0), (0, width - gram.shape[1])))[None]
    v = (kept + swap(given, CORE)).reshape(2, 2, 4, rank, width)
    over_x = swap(jnp.concatenate([v[0, 1], gram]), X)
    v = v[0, 0] + over_x[:4] + swap(v[1, 0], Y) + swap(v[1, 1], X ^ Y)
    gram = gram + over_x[4:]
    v = [jnp.concatenate([v[n : n + 1], gram]) for n in range(4)]
    v = (v[0] + swap(v[1], Z_LOW)) + (swap(v[2], Z_HIGH) + swap(v[3], Z_LOW ^ Z_HIGH))
    v, gram = v[0], v[1, :, :GRAM_LANES]
    v = jnp.stack([v, swap(v, Z_LOW), swap(v, Z_HIGH), swap(v, Z_LOW ^ Z_HIGH)])
    v = jnp.stack([v, swap(v, X), swap(v, Y), swap(v, X ^ Y)])
    v = jnp.stack([v, swap(v, CORE)])
    return v.reshape(PIECES, rank, width), gram


def local(grad, error, q_prev):
    replicas, shards = lax.axis_size("rep"), lax.axis_size("fsdp")
    paired = replicas == 4 and shards == 8
    if paired:
        r, f = lax.axis_index("rep"), lax.axis_index("fsdp")
        place = (r & 1) * 16 + (r >> 1) * 8 + (f & 1) * 4 + (f >> 1)
    else:
        place = 0
    place = jnp.asarray(place, jnp.int32).reshape(1)
    high, low, pt = correct(place, grad, error, q_prev.T)
    if paired:
        pt = pt + swap(pt, CORE)
        pt = pt + swap(pt, Y)
        half = PIECES // 2
        given, gram, mean = terms_of(place, pt, high, low, replicas, half, half, True)
        (kept,) = terms_of(place, pt, high, low, replicas, 0, half, False)
        sums, gram = all_sum(kept, given, gram)
    else:
        pt = lax.psum(pt, "rep")
        terms, gram, mean = terms_of(place, pt, high, low, replicas, 0, PIECES, True)
        sums, gram = lax.psum(terms, AXES), lax.psum(gram, "fsdp")
    inverse, left = factor(gram, mean)
    new_error, update, qt = update_of(place, sums, inverse, left, high, low, replicas)
    return update, new_error, qt.T


def solution(mesh):
    placed = (P("rep", "fsdp", None), P("rep", "fsdp", None), P())
    return jax.shard_map(
        local,
        mesh=mesh,
        in_specs=placed,
        out_specs=(P("fsdp", None), P("rep", "fsdp", None), P()),
        check_vma=False,
    )
```

```python
import functools

import jax
import jax.numpy as jnp
from jax import lax
from jax.experimental import pallas as pl
from jax.experimental.pallas import tpu as pltpu
from jax.sharding import PartitionSpec as P

F32, BF16 = jnp.float32, jnp.bfloat16
HIGHEST = lax.Precision.HIGHEST
AXES = ("rep", "fsdp")
NT = (((1,), (1,)), ((), ()))
NN = (((1,), (0,)), ((), ()))
VMEM = pl.BlockSpec(memory_space=pltpu.VMEM)
PIECES = 32
GROUP = PIECES // 8
GRAM_ROWS = 8


def params(mib):
    return pltpu.CompilerParams(vmem_limit_bytes=mib * 2**20)


def cost(microseconds):
    return pl.CostEstimate(flops=int(1e9 * microseconds), bytes_accessed=int(3.5e6 * microseconds), transcendentals=0)


def in_vmem(x):
    return pltpu.with_memory_space_constraint(x, pltpu.VMEM)


def in_hbm(x):
    return pltpu.with_memory_space_constraint(x, pltpu.HBM)


def two(x):
    high = x.astype(BF16)
    return high, (x - high.astype(F32)).astype(BF16)


def dot(a, b, dims=NN, precision=None):
    return lax.dot_general(a, b, dims, precision=precision, preferred_element_type=F32)


def correct_kernel(parts, grad, error, qt, high, low, pt, grads, errors, factors, total, sems):
    rows, cols = high.shape
    rank = qt.shape[0]
    width = cols // parts
    takes = []
    for part in range(parts):
        columns = pl.ds(part * width, width)
        takes.append(
            (
                pltpu.make_async_copy(error.at[0, :, columns], errors.at[:, columns], sems.at[0, part]),
                pltpu.make_async_copy(grad.at[0, :, columns], grads.at[:, columns], sems.at[1, part]),
                pltpu.make_async_copy(qt.at[:, columns], factors.at[:, columns], sems.at[2, part]),
            )
        )
        for take in takes[-1]:
            take.start()
    total[...] = jnp.zeros_like(total)
    for part in range(parts):
        columns = pl.ds(part * width, width)
        for take in takes[part]:
            take.wait()
        hi, lo = two(grads[:, columns].astype(F32) + errors[:, columns])
        high[:, columns] = hi
        low[:, columns] = lo
        qh, ql = two(factors[:, columns])
        a = dot(jnp.concatenate([qh, ql], 0), hi, NT)
        total[...] += a[:rank] + a[rank:] + dot(qh, lo, NT)
    pt[...] = total[...]


def correct(grad, error, qt):
    _, rows, cols = grad.shape
    rank = qt.shape[0]
    parts = cols // 512
    return pl.pallas_call(
        functools.partial(correct_kernel, parts),
        in_specs=[pl.BlockSpec(memory_space=pltpu.HBM)] * 3,
        out_specs=[VMEM, VMEM, VMEM],
        out_shape=[
            pltpu.VMEM((rows, cols), BF16),
            pltpu.VMEM((rows, cols), BF16),
            pltpu.VMEM((rank, rows), F32),
        ],
        scratch_shapes=[
            pltpu.VMEM((rows, cols), BF16),
            pltpu.VMEM((rows, cols), F32),
            pltpu.VMEM((rank, cols), F32),
            pltpu.VMEM((rank, rows), F32),
            pltpu.SemaphoreType.DMA((3, parts)),
        ],
        compiler_params=params(32),
        name="correct",
    )(in_hbm(grad), in_hbm(error), in_hbm(qt))


def terms_kernel(replicas, first, paired, pt, high, low, earlier, terms, mean=None):
    rank = pt.shape[0]
    width = high.shape[1] // PIECES
    pm = pt[...] / replicas
    ph, pl_ = two(pm)
    both = jnp.concatenate([ph, pl_], 0)
    here = first_piece(paired)
    if mean is None:
        gram = jnp.zeros((GRAM_ROWS, 128), F32)
    else:
        mean[...] = pm
        g = dot(pm, pm, NT, HIGHEST)
        gram = jnp.concatenate([g[n : n + GRAM_ROWS] for n in range(0, rank, GRAM_ROWS)], 1)
    at = 0
    for n in range(terms.shape[0] // (GROUP * rank * (width // 128))):
        for m in range(GROUP):
            columns = pl.ds(pl.multiple_of(((first + n * GROUP + m) ^ here) * width, width), width)
            a = dot(both, high[:, columns])
            a = a[:rank] + a[rank:] + dot(ph, low[:, columns])
            for k in range(0, width, 128):
                terms[at : at + rank] = a[:, k : k + 128]
                at += rank
        terms[at : at + GRAM_ROWS] = gram
        at += GRAM_ROWS


def terms_of(paired, pt, high, low, replicas, first, pieces, earlier, last):
    rank, rows = pt.shape
    tall = pieces * rank * (high.shape[1] // PIECES // 128) + pieces // GROUP * GRAM_ROWS
    shapes = [pltpu.VMEM((tall, 128), F32)] + [pltpu.VMEM((rank, rows), F32)] * last
    return pl.pallas_call(
        functools.partial(terms_kernel, replicas, first, paired),
        in_specs=[VMEM] * 4,
        out_specs=[VMEM] * len(shapes),
        out_shape=shapes,
        compiler_params=params(2),
        cost_estimate=cost(0.1 * pieces),
        name="terms",
    )(pt, in_vmem(high), in_vmem(low), earlier)


def factor_kernel(paired, gram, other, mean, inverse, left):
    rank, rows = mean.shape
    i = lax.broadcasted_iota(jnp.int32, (rank, 2 * rank), 0)
    j = lax.broadcasted_iota(jnp.int32, (rank, 2 * rank), 1)
    gram = gram[...]
    if paired:
        gram = jnp.where((lax.axis_index("rep") & 1) == 0, gram, other[...]) / 2
    total = jnp.concatenate([gram[:, n * rank : (n + 1) * rank] for n in range(rank // GRAM_ROWS)], 0)
    total = jnp.concatenate([total, jnp.zeros_like(total)], 1)
    diagonal = jnp.where(i == j, total, 0.0)
    trace = jnp.sum(jnp.sum(diagonal, 1, keepdims=True), 0, keepdims=True)
    shift = 0.001 * trace / rank
    work = total + jnp.where(i == j, shift, 0.0) + jnp.where(j == i + rank, 1.0, 0.0)
    scale = jnp.zeros((rank, 2 * rank), F32)
    for first in range(0, rank, 8):
        spread = [jnp.broadcast_to(work[:, k : k + 1], work.shape) for k in range(first, first + 8)]
        for n in range(8):
            k = first + n
            column = spread[n]
            value = column[k : k + 1]
            scale = jnp.where(i == k, lax.rsqrt(value), scale)
            ratio = jnp.where(i > k, column / value, 0.0)
            work = work - ratio * work[k : k + 1]
            for m in range(n + 1, 8):
                spread[m] = spread[m] - ratio * spread[m][k : k + 1]
    w = (work * scale)[:, rank:]
    inverse[...] = w
    hat = dot(w, mean[...], NN, HIGHEST).T
    h, l = two(hat)
    left[...] = jnp.concatenate([h, l, h, jnp.zeros((rows, 128 - 3 * rank), BF16)], 1)


def factor(paired, gram, other, mean):
    rank, rows = mean.shape
    return pl.pallas_call(
        functools.partial(factor_kernel, paired),
        in_specs=[VMEM] * 3,
        out_specs=[VMEM, VMEM],
        out_shape=[pltpu.VMEM((rank, rank), F32), pltpu.VMEM((rows, 128), BF16)],
        compiler_params=params(2),
        cost_estimate=cost(1.5),
        name="factor",
    )(gram, other, mean)


def update_kernel(replicas, spots, arrays, paired, inverse, left, high, low, *refs):
    new_error, update, qt, zero, errors, updates, factors, sems = refs[-8:]
    zero[...] = jnp.zeros_like(zero)
    count = len(spots)
    rank = inverse.shape[0]
    width = high.shape[1] // PIECES
    tall = rank * (width // 128)
    here = first_piece(paired)
    groups = [ref.at[n : n + GROUP * tall] for ref in refs[:arrays] for n in range(0, ref.shape[0], GROUP * tall)]
    gives = []
    for g in range(count):
        for n in range(GROUP):
            at = g * GROUP + n
            columns = pl.ds(pl.multiple_of(((spots[g] * GROUP + n) ^ here) * width, width), width)
            sums = jnp.concatenate([groups[g][k : k + rank] for k in range(n * tall, (n + 1) * tall, rank)], 1)
            q = dot(inverse[...], sums, NN, HIGHEST) / replicas
            factors[at] = q
            h, l = two(q)
            right = jnp.concatenate([h, h, l, jnp.zeros((128 - 3 * rank, width), BF16)], 0)
            approx = dot(left[...], right)
            updates[at] = approx.astype(BF16)
            errors[at] = (high[:, columns].astype(F32) - approx) + low[:, columns].astype(F32)
            for k, (source, target) in enumerate(
                ((errors, new_error.at[0, :, columns]), (updates, update.at[:, columns]), (factors, qt.at[:, columns]))
            ):
                gives.append(pltpu.make_async_copy(source.at[at], target, sems.at[k, at]))
                gives[-1].start()
    for give in gives:
        give.wait()


def update_of(paired, groups, spots, inverse, left, high, low, replicas, outs):
    rank = inverse.shape[0]
    rows, cols = high.shape
    count = len(groups)
    width = cols // PIECES
    pieces = len(spots) * GROUP
    fixed = 4 + count
    return pl.pallas_call(
        functools.partial(update_kernel, replicas, tuple(spots), len(groups), paired),
        in_specs=[VMEM] * (4 + count) + [pl.BlockSpec(memory_space=pltpu.HBM)] * len(outs),
        out_specs=[pl.BlockSpec(memory_space=pltpu.HBM)] * 3 + [VMEM],
        out_shape=[
            jax.ShapeDtypeStruct((1, rows, cols), F32),
            jax.ShapeDtypeStruct((rows, cols), BF16),
            jax.ShapeDtypeStruct((rank, cols), F32),
            pltpu.VMEM((8, 128), F32),
        ],
        input_output_aliases={fixed + n: n for n in range(len(outs))},
        scratch_shapes=[
            pltpu.VMEM((pieces, rows, width), F32),
            pltpu.VMEM((pieces, rows, width), BF16),
            pltpu.VMEM((pieces, rank, width), F32),
            pltpu.SemaphoreType.DMA((3, pieces)),
        ],
        compiler_params=params(pieces + 2),
        cost_estimate=cost(1 + 0.3 * pieces),
        name="update",
    )(inverse, left, in_vmem(high), in_vmem(low), *map(in_vmem, groups), *outs)


def first_piece(paired):
    if not paired:
        return 0
    r, f = lax.axis_index("rep"), lax.axis_index("fsdp")
    return GROUP * ((r & 1) * 4 + (r >> 1) * 2 + (f & 1))


def swap(x, mask, mask_one=None):
    devices = lax.axis_size("rep") * lax.axis_size("fsdp")
    masks = (mask, mask if mask_one is None else mask_one)
    return lax.ppermute(x, AXES, [(i, i ^ masks[i // CORE & 1]) for i in range(devices)])


CORE, Y, X, Z_LOW, Z_HIGH = 8, 16, 1, 2, 4


def paired_step(grad, error, qt, replicas):
    high, low, pt = correct(grad, error, qt)
    pt = pt + swap(pt, CORE)
    pt = pt + swap(pt, Y)
    half = PIECES // 2
    (given,) = terms_of(True, pt, high, low, replicas, half, half, pt, False)
    kept, mean = terms_of(True, pt, high, low, replicas, GROUP, half - GROUP, given, True)
    own, _ = terms_of(True, pt, high, low, replicas, 0, GROUP, kept, True)
    given = jnp.split(swap(given, CORE), [own.shape[0]])
    sums = [own + given[0]] + jnp.split(kept + given[1], 3)
    from_x, from_y, from_xy = swap(sums[1], X), swap(sums[2], Y), swap(sums[3], X ^ Y)
    own = (from_xy + from_y) + (from_x + sums[0])
    own = own + swap(own, Z_LOW, Z_HIGH)
    own = own + swap(own, Z_HIGH, Z_LOW)
    tall = own.shape[0] - GRAM_ROWS
    other = swap(own, CORE)
    own, gram = own[:tall], own[tall:]
    from_x, from_y, from_xy = swap(own, X), swap(own, Y), swap(own, X ^ Y)
    inverse, left = factor(True, gram, other[tall:], mean)
    *outs, zero = update_of(True, (own, other[:tall]), (0, 4), inverse, left, high, low, replicas, ())
    rest = jnp.concatenate([from_x, from_y, from_xy])
    others = swap(rest + zero[:1], CORE)
    *outs, _ = update_of(True, (from_x, from_y, from_xy), (1, 2, 3), inverse, left, high, low, replicas, outs)
    *outs, _ = update_of(True, (others,), (5, 6, 7), inverse, left, high, low, replicas, outs)
    return outs


def plain_step(grad, error, qt, replicas):
    high, low, pt = correct(grad, error, qt)
    pt = lax.psum(pt, "rep")
    terms, mean = terms_of(False, pt, high, low, replicas, 0, PIECES, pt, True)
    groups = jnp.split(lax.psum(terms, AXES), PIECES // GROUP)
    tall = groups[0].shape[0] - GRAM_ROWS
    gram = groups[0][tall:] / replicas
    inverse, left = factor(False, gram, gram, mean)
    groups = [group[:tall] for group in groups]
    *outs, _ = update_of(False, groups, range(len(groups)), inverse, left, high, low, replicas, ())
    return outs


def local(grad, error, q_prev):
    replicas, shards = lax.axis_size("rep"), lax.axis_size("fsdp")
    step = paired_step if (replicas, shards) == (4, 8) else plain_step
    new_error, update, qt = step(grad, error, q_prev.T, replicas)
    return update, new_error, qt.T


def solution(mesh):
    placed = (P("rep", "fsdp", None), P("rep", "fsdp", None), P())
    return jax.shard_map(
        local,
        mesh=mesh,
        in_specs=placed,
        out_specs=(P("fsdp", None), P("rep", "fsdp", None), P()),
        check_vma=False,
    )
```

```python
import functools

import jax
import jax.numpy as jnp
from jax import lax
from jax.experimental import pallas as pl
from jax.experimental.pallas import tpu as pltpu
from jax.sharding import PartitionSpec as P

F32, BF16 = jnp.float32, jnp.bfloat16
HIGHEST = lax.Precision.HIGHEST
AXES = ("rep", "fsdp")
NT = (((1,), (1,)), ((), ()))
NN = (((1,), (0,)), ((), ()))
VMEM = pl.BlockSpec(memory_space=pltpu.VMEM)
PIECES = 32
GROUP = PIECES // 8
GRAM_ROWS = 8


def params(mib):
    return pltpu.CompilerParams(vmem_limit_bytes=mib * 2**20)


def cost(microseconds):
    return pl.CostEstimate(flops=int(1e9 * microseconds), bytes_accessed=int(3.5e6 * microseconds), transcendentals=0)


def in_vmem(x):
    return pltpu.with_memory_space_constraint(x, pltpu.VMEM)


def in_hbm(x):
    return pltpu.with_memory_space_constraint(x, pltpu.HBM)


def two(x):
    high = x.astype(BF16)
    return high, (x - high.astype(F32)).astype(BF16)


def dot(a, b, dims=NN, precision=None):
    return lax.dot_general(a, b, dims, precision=precision, preferred_element_type=F32)


def correct_kernel(parts, grad, error, qt, high, low, pt, grads, errors, factors, total, sems):
    rows, cols = high.shape
    rank = qt.shape[0]
    width = cols // parts
    takes = []
    for part in range(parts):
        columns = pl.ds(part * width, width)
        takes.append(
            (
                pltpu.make_async_copy(error.at[0, :, columns], errors.at[:, columns], sems.at[0, part]),
                pltpu.make_async_copy(grad.at[0, :, columns], grads.at[:, columns], sems.at[1, part]),
                pltpu.make_async_copy(qt.at[:, columns], factors.at[:, columns], sems.at[2, part]),
            )
        )
        for take in takes[-1]:
            take.start()
    total[...] = jnp.zeros_like(total)
    for part in range(parts):
        columns = pl.ds(part * width, width)
        for take in takes[part]:
            take.wait()
        hi, lo = two(grads[:, columns].astype(F32) + errors[:, columns])
        high[:, columns] = hi
        low[:, columns] = lo
        qh, ql = two(factors[:, columns])
        a = dot(jnp.concatenate([qh, ql], 0), hi, NT)
        total[...] += a[:rank] + a[rank:] + dot(qh, lo, NT)
    pt[...] = total[...]


def correct(grad, error, qt):
    _, rows, cols = grad.shape
    rank = qt.shape[0]
    parts = cols // 512
    return pl.pallas_call(
        functools.partial(correct_kernel, parts),
        in_specs=[pl.BlockSpec(memory_space=pltpu.HBM)] * 3,
        out_specs=[VMEM, VMEM, VMEM],
        out_shape=[
            pltpu.VMEM((rows, cols), BF16),
            pltpu.VMEM((rows, cols), BF16),
            pltpu.VMEM((rank, rows), F32),
        ],
        scratch_shapes=[
            pltpu.VMEM((rows, cols), BF16),
            pltpu.VMEM((rows, cols), F32),
            pltpu.VMEM((rank, cols), F32),
            pltpu.VMEM((rank, rows), F32),
            pltpu.SemaphoreType.DMA((3, parts)),
        ],
        compiler_params=params(32),
        name="correct",
    )(in_hbm(grad), in_hbm(error), in_hbm(qt))


def terms_kernel(replicas, first, paired, with_gram, pt, high, low, earlier, terms, *mean):
    rank = pt.shape[0]
    width = high.shape[1] // PIECES
    pm = pt[...] / replicas
    ph, pl_ = two(pm)
    both = jnp.concatenate([ph, pl_], 0)
    here = first_piece(paired)
    if mean:
        mean[0][...] = pm
    gram = jnp.zeros((GRAM_ROWS, 128), F32)
    if with_gram:
        g = dot(pm, pm, NT, HIGHEST)
        gram = jnp.concatenate([g[n : n + GRAM_ROWS] for n in range(0, rank, GRAM_ROWS)], 1)
    at = 0
    for n in range(terms.shape[0] // (GROUP * rank * (width // 128))):
        for m in range(GROUP):
            columns = pl.ds(pl.multiple_of(((first + n * GROUP + m) ^ here) * width, width), width)
            a = dot(both, high[:, columns])
            a = a[:rank] + a[rank:] + dot(ph, low[:, columns])
            for k in range(0, width, 128):
                terms[at : at + rank] = a[:, k : k + 128]
                at += rank
        terms[at : at + GRAM_ROWS] = gram
        at += GRAM_ROWS


def terms_of(paired, pt, high, low, replicas, first, pieces, earlier, with_gram=False, with_mean=False):
    rank, rows = pt.shape
    tall = pieces * rank * (high.shape[1] // PIECES // 128) + pieces // GROUP * GRAM_ROWS
    shapes = [pltpu.VMEM((tall, 128), F32)] + [pltpu.VMEM((rank, rows), F32)] * with_mean
    return pl.pallas_call(
        functools.partial(terms_kernel, replicas, first, paired, with_gram),
        in_specs=[VMEM] * 4,
        out_specs=[VMEM] * len(shapes),
        out_shape=shapes,
        compiler_params=params(2),
        cost_estimate=cost(0.1 * pieces),
        name="terms",
    )(pt, in_vmem(high), in_vmem(low), earlier)


def factor_kernel(paired, gram, other, mean, inverse, left):
    rank, rows = mean.shape
    i = lax.broadcasted_iota(jnp.int32, (rank, 2 * rank), 0)
    j = lax.broadcasted_iota(jnp.int32, (rank, 2 * rank), 1)
    gram = gram[...]
    if paired:
        gram = jnp.where((lax.axis_index("rep") & 1) == 0, gram, other[...]) / 2
    total = jnp.concatenate([gram[:, n * rank : (n + 1) * rank] for n in range(rank // GRAM_ROWS)], 0)
    total = jnp.concatenate([total, jnp.zeros_like(total)], 1)
    diagonal = jnp.where(i == j, total, 0.0)
    trace = jnp.sum(jnp.sum(diagonal, 1, keepdims=True), 0, keepdims=True)
    shift = 0.001 * trace / rank
    work = total + jnp.where(i == j, shift, 0.0) + jnp.where(j == i + rank, 1.0, 0.0)
    scale = jnp.zeros((rank, 2 * rank), F32)
    for first in range(0, rank, 8):
        spread = [jnp.broadcast_to(work[:, k : k + 1], work.shape) for k in range(first, first + 8)]
        for n in range(8):
            k = first + n
            column = spread[n]
            value = column[k : k + 1]
            scale = jnp.where(i == k, lax.rsqrt(value), scale)
            ratio = jnp.where(i > k, column / value, 0.0)
            work = work - ratio * work[k : k + 1]
            for m in range(n + 1, 8):
                spread[m] = spread[m] - ratio * spread[m][k : k + 1]
    w = (work * scale)[:, rank:]
    inverse[...] = w
    hat = dot(w, mean[...], NN, HIGHEST).T
    h, l = two(hat)
    left[...] = jnp.concatenate([h, l, h, jnp.zeros((rows, 128 - 3 * rank), BF16)], 1)


def factor(paired, gram, other, mean):
    rank, rows = mean.shape
    return pl.pallas_call(
        functools.partial(factor_kernel, paired),
        in_specs=[VMEM] * 3,
        out_specs=[VMEM, VMEM],
        out_shape=[pltpu.VMEM((rank, rank), F32), pltpu.VMEM((rows, 128), BF16)],
        compiler_params=params(2),
        cost_estimate=cost(1.5),
        name="factor",
    )(gram, other, mean)


def update_kernel(replicas, spots, arrays, paired, with_zero, inverse, left, high, low, *refs):
    new_error, update, qt, *zero, errors, updates, factors, sems = refs[-7 - with_zero :]
    if with_zero:
        zero[0][...] = jnp.zeros_like(zero[0])
    count = len(spots)
    rank = inverse.shape[0]
    width = high.shape[1] // PIECES
    tall = rank * (width // 128)
    here = first_piece(paired)
    groups = [ref.at[n : n + GROUP * tall] for ref in refs[:arrays] for n in range(0, ref.shape[0], GROUP * tall)]
    gives = []
    for g in range(count):
        for n in range(GROUP):
            at = g * GROUP + n
            columns = pl.ds(pl.multiple_of(((spots[g] * GROUP + n) ^ here) * width, width), width)
            sums = jnp.concatenate([groups[g][k : k + rank] for k in range(n * tall, (n + 1) * tall, rank)], 1)
            q = dot(inverse[...], sums, NN, HIGHEST) / replicas
            factors[at] = q
            h, l = two(q)
            right = jnp.concatenate([h, h, l, jnp.zeros((128 - 3 * rank, width), BF16)], 0)
            approx = dot(left[...], right)
            updates[at] = approx.astype(BF16)
            errors[at] = (high[:, columns].astype(F32) - approx) + low[:, columns].astype(F32)
            for k, (source, target) in enumerate(
                ((errors, new_error.at[0, :, columns]), (updates, update.at[:, columns]), (factors, qt.at[:, columns]))
            ):
                gives.append(pltpu.make_async_copy(source.at[at], target, sems.at[k, at]))
                gives[-1].start()
    for give in gives:
        give.wait()


def update_of(paired, groups, spots, inverse, left, high, low, replicas, outs, with_zero=False):
    rank = inverse.shape[0]
    rows, cols = high.shape
    count = len(groups)
    width = cols // PIECES
    pieces = len(spots) * GROUP
    fixed = 4 + count
    return pl.pallas_call(
        functools.partial(update_kernel, replicas, tuple(spots), len(groups), paired, with_zero),
        in_specs=[VMEM] * (4 + count) + [pl.BlockSpec(memory_space=pltpu.HBM)] * len(outs),
        out_specs=[pl.BlockSpec(memory_space=pltpu.HBM)] * 3 + [VMEM] * with_zero,
        out_shape=[
            jax.ShapeDtypeStruct((1, rows, cols), F32),
            jax.ShapeDtypeStruct((rows, cols), BF16),
            jax.ShapeDtypeStruct((rank, cols), F32),
        ]
        + [pltpu.VMEM((8, 128), F32)] * with_zero,
        input_output_aliases={fixed + n: n for n in range(len(outs))},
        scratch_shapes=[
            pltpu.VMEM((pieces, rows, width), F32),
            pltpu.VMEM((pieces, rows, width), BF16),
            pltpu.VMEM((pieces, rank, width), F32),
            pltpu.SemaphoreType.DMA((3, pieces)),
        ],
        compiler_params=params(pieces + 2),
        cost_estimate=cost(1 + 0.3 * pieces),
        name="update",
    )(inverse, left, in_vmem(high), in_vmem(low), *map(in_vmem, groups), *outs)


def first_piece(paired):
    if not paired:
        return 0
    r, f = lax.axis_index("rep"), lax.axis_index("fsdp")
    return GROUP * ((r & 1) * 4 + (r >> 1) * 2 + (f & 1))


def swap(x, mask, mask_one=None):
    devices = lax.axis_size("rep") * lax.axis_size("fsdp")
    masks = (mask, mask if mask_one is None else mask_one)
    return lax.ppermute(x, AXES, [(i, i ^ masks[i // CORE & 1]) for i in range(devices)])


CORE, Y, X, Z_LOW, Z_HIGH = 8, 16, 1, 2, 4


def paired_step(grad, error, qt, replicas):
    high, low, pt = correct(grad, error, qt)
    pt = pt + swap(pt, CORE)
    pt = pt + swap(pt, Y)
    half = PIECES // 2
    (given,) = terms_of(True, pt, high, low, replicas, half, half, pt)
    kept, mean = terms_of(True, pt, high, low, replicas, GROUP, half - GROUP, given, True, True)
    (own,) = terms_of(True, pt, high, low, replicas, 0, GROUP, kept, True)
    given = jnp.split(swap(given, CORE), [own.shape[0]])
    sums = [own + given[0]] + jnp.split(kept + given[1], 3)
    from_x, from_y, from_xy = swap(sums[1], X), swap(sums[2], Y), swap(sums[3], X ^ Y)
    own = (from_xy + from_y) + (from_x + sums[0])
    own = own + swap(own, Z_LOW, Z_HIGH)
    own = own + swap(own, Z_HIGH, Z_LOW)
    tall = own.shape[0] - GRAM_ROWS
    other = swap(own, CORE)
    own, gram = own[:tall], own[tall:]
    from_x, from_y, from_xy = swap(own, X), swap(own, Y), swap(own, X ^ Y)
    inverse, left = factor(True, gram, other[tall:], mean)
    *outs, zero = update_of(True, (own, other[:tall]), (0, 4), inverse, left, high, low, replicas, (), True)
    rest = jnp.concatenate([from_x, from_y, from_xy])
    others = swap(rest + zero[:1], CORE)
    outs = update_of(True, (from_x, from_y, from_xy), (1, 2, 3), inverse, left, high, low, replicas, outs)
    outs = update_of(True, (others,), (5, 6, 7), inverse, left, high, low, replicas, outs)
    return outs


def plain_step(grad, error, qt, replicas):
    high, low, pt = correct(grad, error, qt)
    pt = lax.psum(pt, "rep")
    terms, mean = terms_of(False, pt, high, low, replicas, 0, PIECES, pt, True, True)
    groups = jnp.split(lax.psum(terms, AXES), PIECES // GROUP)
    tall = groups[0].shape[0] - GRAM_ROWS
    gram = groups[0][tall:] / replicas
    inverse, left = factor(False, gram, gram, mean)
    groups = [group[:tall] for group in groups]
    outs = update_of(False, groups, range(len(groups)), inverse, left, high, low, replicas, ())
    return outs


def local(grad, error, q_prev):
    replicas, shards = lax.axis_size("rep"), lax.axis_size("fsdp")
    step = paired_step if (replicas, shards) == (4, 8) else plain_step
    new_error, update, qt = step(grad, error, q_prev.T, replicas)
    return update, new_error, qt.T


def solution(mesh):
    placed = (P("rep", "fsdp", None), P("rep", "fsdp", None), P())
    return jax.shard_map(
        local,
        mesh=mesh,
        in_specs=placed,
        out_specs=(P("fsdp", None), P("rep", "fsdp", None), P()),
        check_vma=False,
    )
```

```python
import functools

import jax
import jax.numpy as jnp
from jax import lax
from jax.experimental import pallas as pl
from jax.experimental.pallas import tpu as pltpu
from jax.sharding import PartitionSpec as P

F32, BF16 = jnp.float32, jnp.bfloat16
HIGHEST = lax.Precision.HIGHEST
AXES = ("rep", "fsdp")
NT = (((1,), (1,)), ((), ()))
NN = (((1,), (0,)), ((), ()))
VMEM = pl.BlockSpec(memory_space=pltpu.VMEM)
PIECES = 32
GROUP = PIECES // 8
GRAM_ROWS = 8


def params(mib):
    return pltpu.CompilerParams(vmem_limit_bytes=mib * 2**20)


def cost(microseconds):
    return pl.CostEstimate(flops=int(1e9 * microseconds), bytes_accessed=int(3.5e6 * microseconds), transcendentals=0)


def in_vmem(x):
    return pltpu.with_memory_space_constraint(x, pltpu.VMEM)


def in_hbm(x):
    return pltpu.with_memory_space_constraint(x, pltpu.HBM)


def two(x):
    high = x.astype(BF16)
    return high, (x - high.astype(F32)).astype(BF16)


def dot(a, b, dims=NN, precision=None):
    return lax.dot_general(a, b, dims, precision=precision, preferred_element_type=F32)


def correct_kernel(parts, grad, error, qt, high, low, pt, grads, errors, factors, total, sems):
    rows, cols = high.shape
    rank = qt.shape[0]
    width = cols // parts
    takes = []
    for part in range(parts):
        columns = pl.ds(part * width, width)
        takes.append(
            (
                pltpu.make_async_copy(error.at[0, :, columns], errors.at[:, columns], sems.at[0, part]),
                pltpu.make_async_copy(grad.at[0, :, columns], grads.at[:, columns], sems.at[1, part]),
                pltpu.make_async_copy(qt.at[:, columns], factors.at[:, columns], sems.at[2, part]),
            )
        )
        for take in takes[-1]:
            take.start()
    total[...] = jnp.zeros_like(total)
    for part in range(parts):
        columns = pl.ds(part * width, width)
        for take in takes[part]:
            take.wait()
        hi, lo = two(grads[:, columns].astype(F32) + errors[:, columns])
        high[:, columns] = hi
        low[:, columns] = lo
        qh, ql = two(factors[:, columns])
        a = dot(jnp.concatenate([qh, ql], 0), hi, NT)
        total[...] += a[:rank] + a[rank:] + dot(qh, lo, NT)
    pt[...] = total[...]


def correct(grad, error, qt):
    _, rows, cols = grad.shape
    rank = qt.shape[0]
    parts = cols // 512
    return pl.pallas_call(
        functools.partial(correct_kernel, parts),
        in_specs=[pl.BlockSpec(memory_space=pltpu.HBM)] * 3,
        out_specs=[VMEM, VMEM, VMEM],
        out_shape=[
            pltpu.VMEM((rows, cols), BF16),
            pltpu.VMEM((rows, cols), BF16),
            pltpu.VMEM((rank, rows), F32),
        ],
        scratch_shapes=[
            pltpu.VMEM((rows, cols), BF16),
            pltpu.VMEM((rows, cols), F32),
            pltpu.VMEM((rank, cols), F32),
            pltpu.VMEM((rank, rows), F32),
            pltpu.SemaphoreType.DMA((3, parts)),
        ],
        compiler_params=params(32),
        name="correct",
    )(in_hbm(grad), in_hbm(error), in_hbm(qt))


def terms_kernel(replicas, first, paired, with_gram, pt, high, low, earlier, terms, *mean):
    rank = pt.shape[0]
    width = high.shape[1] // PIECES
    pm = pt[...] / replicas
    ph, pl_ = two(pm)
    both = jnp.concatenate([ph, pl_], 0)
    here = first_piece(paired)
    if mean:
        mean[0][...] = pm
    gram = jnp.zeros((GRAM_ROWS, 128), F32)
    if with_gram:
        g = dot(pm, pm, NT, HIGHEST)
        gram = jnp.concatenate([g[n : n + GRAM_ROWS] for n in range(0, rank, GRAM_ROWS)], 1)
    at = 0
    for n in range(terms.shape[0] // (GROUP * rank * (width // 128))):
        for m in range(GROUP):
            columns = pl.ds(pl.multiple_of(((first + n * GROUP + m) ^ here) * width, width), width)
            a = dot(both, high[:, columns])
            a = a[:rank] + a[rank:] + dot(ph, low[:, columns])
            for k in range(0, width, 128):
                terms[at : at + rank] = a[:, k : k + 128]
                at += rank
        terms[at : at + GRAM_ROWS] = gram
        at += GRAM_ROWS


def terms_of(paired, pt, high, low, replicas, first, pieces, earlier, with_gram=False, with_mean=False):
    rank, rows = pt.shape
    tall = pieces * rank * (high.shape[1] // PIECES // 128) + pieces // GROUP * GRAM_ROWS
    shapes = [pltpu.VMEM((tall, 128), F32)] + [pltpu.VMEM((rank, rows), F32)] * with_mean
    return pl.pallas_call(
        functools.partial(terms_kernel, replicas, first, paired, with_gram),
        in_specs=[VMEM] * 4,
        out_specs=[VMEM] * len(shapes),
        out_shape=shapes,
        compiler_params=params(2),
        cost_estimate=cost(0.1 * pieces),
        name="terms",
    )(pt, in_vmem(high), in_vmem(low), earlier)


def factor_kernel(paired, gram, other, mean, inverse, left):
    rank, rows = mean.shape
    i = lax.broadcasted_iota(jnp.int32, (rank, 2 * rank), 0)
    j = lax.broadcasted_iota(jnp.int32, (rank, 2 * rank), 1)
    gram = gram[...]
    if paired:
        gram = jnp.where((lax.axis_index("rep") & 1) == 0, gram, other[...]) / 2
    total = jnp.concatenate([gram[:, n * rank : (n + 1) * rank] for n in range(rank // GRAM_ROWS)], 0)
    total = jnp.concatenate([total, jnp.zeros_like(total)], 1)
    diagonal = jnp.where(i == j, total, 0.0)
    trace = jnp.sum(jnp.sum(diagonal, 1, keepdims=True), 0, keepdims=True)
    shift = 0.001 * trace / rank
    work = total + jnp.where(i == j, shift, 0.0) + jnp.where(j == i + rank, 1.0, 0.0)
    scale = jnp.zeros((rank, 2 * rank), F32)
    for first in range(0, rank, 8):
        spread = [jnp.broadcast_to(work[:, k : k + 1], work.shape) for k in range(first, first + 8)]
        for n in range(8):
            k = first + n
            column = spread[n]
            value = column[k : k + 1]
            scale = jnp.where(i == k, lax.rsqrt(value), scale)
            ratio = jnp.where(i > k, column / value, 0.0)
            work = work - ratio * work[k : k + 1]
            for m in range(n + 1, 8):
                spread[m] = spread[m] - ratio * spread[m][k : k + 1]
    w = (work * scale)[:, rank:]
    inverse[...] = w
    hat = dot(w, mean[...], NN, HIGHEST).T
    h, l = two(hat)
    left[...] = jnp.concatenate([h, l, h, jnp.zeros((rows, 128 - 3 * rank), BF16)], 1)


def factor(paired, gram, other, mean):
    rank, rows = mean.shape
    return pl.pallas_call(
        functools.partial(factor_kernel, paired),
        in_specs=[VMEM] * 3,
        out_specs=[VMEM, VMEM],
        out_shape=[pltpu.VMEM((rank, rank), F32), pltpu.VMEM((rows, 128), BF16)],
        compiler_params=params(2),
        cost_estimate=cost(1.5),
        name="factor",
    )(gram, other, mean)


def update_kernel(replicas, spots, arrays, paired, with_zero, inverse, left, high, low, *refs):
    new_error, update, qt, *zero, errors, updates, factors, sems = refs[-7 - with_zero :]
    if with_zero:
        zero[0][...] = jnp.zeros_like(zero[0])
    count = len(spots)
    rank = inverse.shape[0]
    width = high.shape[1] // PIECES
    tall = rank * (width // 128)
    here = first_piece(paired)
    groups = [ref.at[n : n + GROUP * tall] for ref in refs[:arrays] for n in range(0, ref.shape[0], GROUP * tall)]
    gives = []
    for g in range(count):
        for n in range(GROUP):
            at = g * GROUP + n
            columns = pl.ds(pl.multiple_of(((spots[g] * GROUP + n) ^ here) * width, width), width)
            sums = jnp.concatenate([groups[g][k : k + rank] for k in range(n * tall, (n + 1) * tall, rank)], 1)
            q = dot(inverse[...], sums, NN, HIGHEST) / replicas
            factors[at] = q
            h, l = two(q)
            right = jnp.concatenate([h, h, l, jnp.zeros((128 - 3 * rank, width), BF16)], 0)
            approx = dot(left[...], right)
            updates[at] = approx.astype(BF16)
            errors[at] = (high[:, columns].astype(F32) - approx) + low[:, columns].astype(F32)
            for k, (source, target) in enumerate(
                ((errors, new_error.at[0, :, columns]), (updates, update.at[:, columns]), (factors, qt.at[:, columns]))
            ):
                gives.append(pltpu.make_async_copy(source.at[at], target, sems.at[k, at]))
                gives[-1].start()
    for give in gives:
        give.wait()


def update_of(paired, groups, spots, inverse, left, high, low, replicas, outs, with_zero=False):
    rank = inverse.shape[0]
    rows, cols = high.shape
    count = len(groups)
    width = cols // PIECES
    pieces = len(spots) * GROUP
    fixed = 4 + count
    return pl.pallas_call(
        functools.partial(update_kernel, replicas, tuple(spots), len(groups), paired, with_zero),
        in_specs=[VMEM] * (4 + count) + [pl.BlockSpec(memory_space=pltpu.HBM)] * len(outs),
        out_specs=[pl.BlockSpec(memory_space=pltpu.HBM)] * 3 + [VMEM] * with_zero,
        out_shape=[
            jax.ShapeDtypeStruct((1, rows, cols), F32),
            jax.ShapeDtypeStruct((rows, cols), BF16),
            jax.ShapeDtypeStruct((rank, cols), F32),
        ]
        + [pltpu.VMEM((8, 128), F32)] * with_zero,
        input_output_aliases={fixed + n: n for n in range(len(outs))},
        scratch_shapes=[
            pltpu.VMEM((pieces, rows, width), F32),
            pltpu.VMEM((pieces, rows, width), BF16),
            pltpu.VMEM((pieces, rank, width), F32),
            pltpu.SemaphoreType.DMA((3, pieces)),
        ],
        compiler_params=params(pieces + 2),
        cost_estimate=cost(1 + 0.3 * pieces),
        name="update",
    )(inverse, left, in_vmem(high), in_vmem(low), *map(in_vmem, groups), *outs)


def first_piece(paired):
    if not paired:
        return 0
    r, f = lax.axis_index("rep"), lax.axis_index("fsdp")
    return GROUP * ((r & 1) * 4 + (r >> 1) * 2 + (f & 1))


def swap(x, mask, mask_one=None):
    devices = lax.axis_size("rep") * lax.axis_size("fsdp")
    masks = (mask, mask if mask_one is None else mask_one)
    return lax.ppermute(x, AXES, [(i, i ^ masks[i // CORE & 1]) for i in range(devices)])


CORE, Y, X, Z_LOW, Z_HIGH = 8, 16, 1, 2, 4


def paired_step(grad, error, qt, replicas):
    high, low, pt = correct(grad, error, qt)
    pt = pt + swap(pt, CORE)
    pt = pt + swap(pt, Y)
    half = PIECES // 2
    (given,) = terms_of(True, pt, high, low, replicas, half + GROUP, half - GROUP, pt)
    kept, mean = terms_of(True, pt, high, low, replicas, GROUP, half - GROUP, given, True, True)
    at_x, at_y, at_xy = jnp.split(kept + swap(given, CORE), 3)
    from_x, from_y, from_xy = swap(at_x, X), swap(at_y, Y), swap(at_xy, X ^ Y)
    (late,) = terms_of(True, pt, high, low, replicas, half, GROUP, from_xy)
    (own,) = terms_of(True, pt, high, low, replicas, 0, GROUP, late, True)
    own = (from_xy + from_y) + (from_x + (own + swap(late, CORE)))
    own = own + swap(own, Z_LOW, Z_HIGH)
    own = own + swap(own, Z_HIGH, Z_LOW)
    tall = own.shape[0] - GRAM_ROWS
    other = swap(own, CORE)
    own, gram = own[:tall], own[tall:]
    from_x, from_y, from_xy = swap(own, X), swap(own, Y), swap(own, X ^ Y)
    inverse, left = factor(True, gram, other[tall:], mean)
    *outs, zero = update_of(True, (own, other[:tall]), (0, 4), inverse, left, high, low, replicas, (), True)
    rest = jnp.concatenate([from_x, from_y, from_xy])
    others = swap(rest + zero[:1], CORE)
    outs = update_of(True, (from_x, from_y, from_xy), (1, 2, 3), inverse, left, high, low, replicas, outs)
    outs = update_of(True, (others,), (5, 6, 7), inverse, left, high, low, replicas, outs)
    return outs


def plain_step(grad, error, qt, replicas):
    high, low, pt = correct(grad, error, qt)
    pt = lax.psum(pt, "rep")
    terms, mean = terms_of(False, pt, high, low, replicas, 0, PIECES, pt, True, True)
    groups = jnp.split(lax.psum(terms, AXES), PIECES // GROUP)
    tall = groups[0].shape[0] - GRAM_ROWS
    gram = groups[0][tall:] / replicas
    inverse, left = factor(False, gram, gram, mean)
    groups = [group[:tall] for group in groups]
    outs = update_of(False, groups, range(len(groups)), inverse, left, high, low, replicas, ())
    return outs


def local(grad, error, q_prev):
    replicas, shards = lax.axis_size("rep"), lax.axis_size("fsdp")
    step = paired_step if (replicas, shards) == (4, 8) else plain_step
    new_error, update, qt = step(grad, error, q_prev.T, replicas)
    return update, new_error, qt.T


def solution(mesh):
    placed = (P("rep", "fsdp", None), P("rep", "fsdp", None), P())
    return jax.shard_map(
        local,
        mesh=mesh,
        in_specs=placed,
        out_specs=(P("fsdp", None), P("rep", "fsdp", None), P()),
        check_vma=False,
    )
```

```python
import functools

import jax
import jax.numpy as jnp
from jax import lax
from jax.experimental import pallas as pl
from jax.experimental.pallas import tpu as pltpu
from jax.sharding import PartitionSpec as P

F32, BF16 = jnp.float32, jnp.bfloat16
HIGHEST = lax.Precision.HIGHEST
AXES = ("rep", "fsdp")
NT = (((1,), (1,)), ((), ()))
NN = (((1,), (0,)), ((), ()))
VMEM = pl.BlockSpec(memory_space=pltpu.VMEM)
PIECES = 32
GROUP = PIECES // 8
GRAM_ROWS = 8


def params(mib):
    return pltpu.CompilerParams(vmem_limit_bytes=mib * 2**20)


def cost(microseconds):
    return pl.CostEstimate(flops=int(1e9 * microseconds), bytes_accessed=int(3.5e6 * microseconds), transcendentals=0)


def in_vmem(x):
    return pltpu.with_memory_space_constraint(x, pltpu.VMEM)


def in_hbm(x):
    return pltpu.with_memory_space_constraint(x, pltpu.HBM)


def two(x):
    high = x.astype(BF16)
    return high, (x - high.astype(F32)).astype(BF16)


def dot(a, b, dims=NN, precision=None):
    return lax.dot_general(a, b, dims, precision=precision, preferred_element_type=F32)


def correct_kernel(parts, grad, error, qt, high, low, pt, grads, errors, factors, total, sems):
    rows, cols = high.shape
    rank = qt.shape[0]
    ends = [512 * n for n in range(1, parts - 1)]
    ends += [ends[-1] + 256 * n for n in range(1, 5)]
    spans = [pl.ds(start, end - start) for start, end in zip([0] + ends, ends)]
    takes = []
    for part, columns in enumerate(spans):
        takes.append(
            (
                pltpu.make_async_copy(error.at[0, :, columns], errors.at[:, columns], sems.at[0, part]),
                pltpu.make_async_copy(grad.at[0, :, columns], grads.at[:, columns], sems.at[1, part]),
                pltpu.make_async_copy(qt.at[:, columns], factors.at[:, columns], sems.at[2, part]),
            )
        )
        for take in takes[-1]:
            take.start()
    total[...] = jnp.zeros_like(total)
    for part, columns in enumerate(spans):
        for take in takes[part]:
            take.wait()
        hi, lo = two(grads[:, columns].astype(F32) + errors[:, columns])
        high[:, columns] = hi
        low[:, columns] = lo
        qh, ql = two(factors[:, columns])
        a = dot(jnp.concatenate([qh, ql], 0), hi, NT)
        total[...] += a[:rank] + a[rank:] + dot(qh, lo, NT)
    pt[...] = total[...]


def correct(grad, error, qt):
    _, rows, cols = grad.shape
    rank = qt.shape[0]
    parts = cols // 512
    return pl.pallas_call(
        functools.partial(correct_kernel, parts),
        in_specs=[pl.BlockSpec(memory_space=pltpu.HBM)] * 3,
        out_specs=[VMEM, VMEM, VMEM],
        out_shape=[
            pltpu.VMEM((rows, cols), BF16),
            pltpu.VMEM((rows, cols), BF16),
            pltpu.VMEM((rank, rows), F32),
        ],
        scratch_shapes=[
            pltpu.VMEM((rows, cols), BF16),
            pltpu.VMEM((rows, cols), F32),
            pltpu.VMEM((rank, cols), F32),
            pltpu.VMEM((rank, rows), F32),
            pltpu.SemaphoreType.DMA((3, parts + 2)),
        ],
        compiler_params=params(32),
        name="correct",
    )(in_hbm(grad), in_hbm(error), in_hbm(qt))


def terms_kernel(replicas, first, paired, with_gram, pt, high, low, earlier, terms, *mean):
    rank = pt.shape[0]
    width = high.shape[1] // PIECES
    pm = pt[...] / replicas
    ph, pl_ = two(pm)
    both = jnp.concatenate([ph, pl_], 0)
    here = first_piece(paired)
    if mean:
        mean[0][...] = pm
    gram = jnp.zeros((GRAM_ROWS, 128), F32)
    if with_gram:
        g = dot(pm, pm, NT, HIGHEST)
        gram = jnp.concatenate([g[n : n + GRAM_ROWS] for n in range(0, rank, GRAM_ROWS)], 1)
    at = 0
    for n in range(terms.shape[0] // (GROUP * rank * (width // 128))):
        for m in range(GROUP):
            columns = pl.ds(pl.multiple_of(((first + n * GROUP + m) ^ here) * width, width), width)
            a = dot(both, high[:, columns])
            a = a[:rank] + a[rank:] + dot(ph, low[:, columns])
            for k in range(0, width, 128):
                terms[at : at + rank] = a[:, k : k + 128]
                at += rank
        terms[at : at + GRAM_ROWS] = gram
        at += GRAM_ROWS


def terms_of(paired, pt, high, low, replicas, first, pieces, earlier, with_gram=False, with_mean=False):
    rank, rows = pt.shape
    tall = pieces * rank * (high.shape[1] // PIECES // 128) + pieces // GROUP * GRAM_ROWS
    shapes = [pltpu.VMEM((tall, 128), F32)] + [pltpu.VMEM((rank, rows), F32)] * with_mean
    return pl.pallas_call(
        functools.partial(terms_kernel, replicas, first, paired, with_gram),
        in_specs=[VMEM] * 4,
        out_specs=[VMEM] * len(shapes),
        out_shape=shapes,
        compiler_params=params(2),
        cost_estimate=cost(0.1 * pieces),
        name="terms",
    )(pt, in_vmem(high), in_vmem(low), earlier)


def factor_kernel(paired, gram, other, mean, inverse, left):
    rank, rows = mean.shape
    i = lax.broadcasted_iota(jnp.int32, (rank, 2 * rank), 0)
    j = lax.broadcasted_iota(jnp.int32, (rank, 2 * rank), 1)
    gram = gram[...]
    if paired:
        gram = jnp.where((lax.axis_index("rep") & 1) == 0, gram, other[...]) / 2
    total = jnp.concatenate([gram[:, n * rank : (n + 1) * rank] for n in range(rank // GRAM_ROWS)], 0)
    total = jnp.concatenate([total, jnp.zeros_like(total)], 1)
    diagonal = jnp.where(i == j, total, 0.0)
    trace = jnp.sum(jnp.sum(diagonal, 1, keepdims=True), 0, keepdims=True)
    shift = 0.001 * trace / rank
    work = total + jnp.where(i == j, shift, 0.0) + jnp.where(j == i + rank, 1.0, 0.0)
    scale = jnp.zeros((rank, 2 * rank), F32)
    for first in range(0, rank, 8):
        spread = [jnp.broadcast_to(work[:, k : k + 1], work.shape) for k in range(first, first + 8)]
        for n in range(8):
            k = first + n
            column = spread[n]
            value = column[k : k + 1]
            scale = jnp.where(i == k, lax.rsqrt(value), scale)
            ratio = jnp.where(i > k, column / value, 0.0)
            work = work - ratio * work[k : k + 1]
            for m in range(n + 1, 8):
                spread[m] = spread[m] - ratio * spread[m][k : k + 1]
    w = (work * scale)[:, rank:]
    inverse[...] = w
    hat = dot(w, mean[...], NN, HIGHEST).T
    h, l = two(hat)
    left[...] = jnp.concatenate([h, l, h, jnp.zeros((rows, 128 - 3 * rank), BF16)], 1)


def factor(paired, gram, other, mean):
    rank, rows = mean.shape
    return pl.pallas_call(
        functools.partial(factor_kernel, paired),
        in_specs=[VMEM] * 3,
        out_specs=[VMEM, VMEM],
        out_shape=[pltpu.VMEM((rank, rank), F32), pltpu.VMEM((rows, 128), BF16)],
        compiler_params=params(2),
        cost_estimate=cost(1.5),
        name="factor",
    )(gram, other, mean)


def update_kernel(replicas, spots, arrays, paired, with_zero, inverse, left, high, low, *refs):
    new_error, update, qt, *zero, errors, updates, factors, sems = refs[-7 - with_zero :]
    if with_zero:
        zero[0][...] = jnp.zeros_like(zero[0])
    count = len(spots)
    rank = inverse.shape[0]
    width = high.shape[1] // PIECES
    tall = rank * (width // 128)
    here = first_piece(paired)
    groups = [ref.at[n : n + GROUP * tall] for ref in refs[:arrays] for n in range(0, ref.shape[0], GROUP * tall)]
    gives = []
    for g in range(count):
        for n in range(GROUP):
            at = g * GROUP + n
            columns = pl.ds(pl.multiple_of(((spots[g] * GROUP + n) ^ here) * width, width), width)
            sums = jnp.concatenate([groups[g][k : k + rank] for k in range(n * tall, (n + 1) * tall, rank)], 1)
            q = dot(inverse[...], sums, NN, HIGHEST) / replicas
            factors[at] = q
            h, l = two(q)
            right = jnp.concatenate([h, h, l, jnp.zeros((128 - 3 * rank, width), BF16)], 0)
            approx = dot(left[...], right)
            updates[at] = approx.astype(BF16)
            errors[at] = (high[:, columns].astype(F32) - approx) + low[:, columns].astype(F32)
            for k, (source, target) in enumerate(
                ((errors, new_error.at[0, :, columns]), (updates, update.at[:, columns]), (factors, qt.at[:, columns]))
            ):
                gives.append(pltpu.make_async_copy(source.at[at], target, sems.at[k, at]))
                gives[-1].start()
    for give in gives:
        give.wait()


def update_of(paired, groups, spots, inverse, left, high, low, replicas, outs, with_zero=False):
    rank = inverse.shape[0]
    rows, cols = high.shape
    count = len(groups)
    width = cols // PIECES
    pieces = len(spots) * GROUP
    fixed = 4 + count
    return pl.pallas_call(
        functools.partial(update_kernel, replicas, tuple(spots), len(groups), paired, with_zero),
        in_specs=[VMEM] * (4 + count) + [pl.BlockSpec(memory_space=pltpu.HBM)] * len(outs),
        out_specs=[pl.BlockSpec(memory_space=pltpu.HBM)] * 3 + [VMEM] * with_zero,
        out_shape=[
            jax.ShapeDtypeStruct((1, rows, cols), F32),
            jax.ShapeDtypeStruct((rows, cols), BF16),
            jax.ShapeDtypeStruct((rank, cols), F32),
        ]
        + [pltpu.VMEM((8, 128), F32)] * with_zero,
        input_output_aliases={fixed + n: n for n in range(len(outs))},
        scratch_shapes=[
            pltpu.VMEM((pieces, rows, width), F32),
            pltpu.VMEM((pieces, rows, width), BF16),
            pltpu.VMEM((pieces, rank, width), F32),
            pltpu.SemaphoreType.DMA((3, pieces)),
        ],
        compiler_params=params(pieces + 2),
        cost_estimate=cost(1 + 0.3 * pieces),
        name="update",
    )(inverse, left, in_vmem(high), in_vmem(low), *map(in_vmem, groups), *outs)


def first_piece(paired):
    if not paired:
        return 0
    r, f = lax.axis_index("rep"), lax.axis_index("fsdp")
    return GROUP * ((r & 1) * 4 + (r >> 1) * 2 + (f & 1))


def swap(x, mask, mask_one=None):
    devices = lax.axis_size("rep") * lax.axis_size("fsdp")
    masks = (mask, mask if mask_one is None else mask_one)
    return lax.ppermute(x, AXES, [(i, i ^ masks[i // CORE & 1]) for i in range(devices)])


CORE, Y, X, Z_LOW, Z_HIGH = 8, 16, 1, 2, 4


def paired_step(grad, error, qt, replicas):
    high, low, pt = correct(grad, error, qt)
    pt = pt + swap(pt, CORE)
    pt = pt + swap(pt, Y)
    half = PIECES // 2
    (given,) = terms_of(True, pt, high, low, replicas, half + GROUP, half - GROUP, pt)
    kept, mean = terms_of(True, pt, high, low, replicas, GROUP, half - GROUP, given, True, True)
    at_x, at_y, at_xy = jnp.split(kept + swap(given, CORE), 3)
    from_x, from_y, from_xy = swap(at_x, X), swap(at_y, Y), swap(at_xy, X ^ Y)
    (late,) = terms_of(True, pt, high, low, replicas, half, GROUP, from_xy)
    (own,) = terms_of(True, pt, high, low, replicas, 0, GROUP, late, True)
    own = (from_xy + from_y) + (from_x + (own + swap(late, CORE)))
    own = own + swap(own, Z_LOW, Z_HIGH)
    own = own + swap(own, Z_HIGH, Z_LOW)
    tall = own.shape[0] - GRAM_ROWS
    other = swap(own, CORE)
    own, gram = own[:tall], own[tall:]
    from_x, from_y, from_xy = swap(own, X), swap(own, Y), swap(own, X ^ Y)
    inverse, left = factor(True, gram, other[tall:], mean)
    *outs, zero = update_of(True, (own, other[:tall]), (0, 4), inverse, left, high, low, replicas, (), True)
    rest = jnp.concatenate([from_x, from_y, from_xy])
    others = swap(rest + zero[:1], CORE)
    outs = update_of(True, (from_x, from_y, from_xy), (1, 2, 3), inverse, left, high, low, replicas, outs)
    outs = update_of(True, (others,), (5, 6, 7), inverse, left, high, low, replicas, outs)
    return outs


def plain_step(grad, error, qt, replicas):
    high, low, pt = correct(grad, error, qt)
    pt = lax.psum(pt, "rep")
    terms, mean = terms_of(False, pt, high, low, replicas, 0, PIECES, pt, True, True)
    groups = jnp.split(lax.psum(terms, AXES), PIECES // GROUP)
    tall = groups[0].shape[0] - GRAM_ROWS
    gram = groups[0][tall:] / replicas
    inverse, left = factor(False, gram, gram, mean)
    groups = [group[:tall] for group in groups]
    outs = update_of(False, groups, range(len(groups)), inverse, left, high, low, replicas, ())
    return outs


def local(grad, error, q_prev):
    replicas, shards = lax.axis_size("rep"), lax.axis_size("fsdp")
    step = paired_step if (replicas, shards) == (4, 8) else plain_step
    new_error, update, qt = step(grad, error, q_prev.T, replicas)
    return update, new_error, qt.T


def solution(mesh):
    placed = (P("rep", "fsdp", None), P("rep", "fsdp", None), P())
    return jax.shard_map(
        local,
        mesh=mesh,
        in_specs=placed,
        out_specs=(P("fsdp", None), P("rep", "fsdp", None), P()),
        check_vma=False,
    )
```
